32 devices in a mesh: dp: 8 (over z, y), ctx: 4 (over x, core).
Axes of the slice: x: 2, y: 2, z: 4, core: 2. Of those that a mesh axis runs over, the one named last changes fastest.
Arguments:
- layer_input: bfloat16 [8, 1024, 8192], P('dp', 'ctx'), may hold values from -0.078125 to 0.078125
- query_rows: bfloat16 [8, 1024, 1024], P('dp', 'ctx'), may hold values from -6 to 6
- key_rows: bfloat16 [8, 1024, 128], P('dp', 'ctx'), may hold values from -6 to 6
- value_rows: bfloat16 [8, 1024, 128], P('dp', 'ctx'), may hold values from -6 to 6
- attn_out: bfloat16 [8, 1024, 1024], P('dp', 'ctx'), may hold values from -6 to 6
- d_attn: bfloat16 [8, 1024, 1024], P('dp', 'ctx'), may hold values from -6 to 6
- log_sum_exp: float32 [8, 8, 1024], P('dp', None, 'ctx')
- block_order: int32 [8], replicated, may hold values from 0 to 7, as said below
Outputs:
- d_query: bfloat16 [8, 1024, 1024], P('dp', 'ctx')
- d_weight: float32 [8192, 256], P(('dp', 'ctx'))
The draws below stay inside these ranges and needn't reach their ends.
Inputs may be any that keep to these rules, and one draw needn't show every extreme that they name: `block_order`: each value appears exactly once.
All inputs are finite; a program needn't handle non-finite values.
Results may differ from the reference program's by a relative error of at most 0.0051.
Values may be sent and summed in bfloat16 or wider, within the bound.
A program may use at most 64 MiB of HBM per device.

```python
import jax
import jax.numpy as jnp
from jax import lax

D = 8192
H = 8
DH = 128
TOK_DEV = 256
SEQ = 1024
BATCH = 8


def shared_order(key):
    return jax.random.permutation(jax.random.fold_in(key, 11), 2 * (SEQ // TOK_DEV)).astype(jnp.int32)


def draw_block_order(key, part):
    return shared_order(key)


def draw_log_sum_exp(key, part):
    order = shared_order(key)
    half = TOK_DEV // 2
    index = jnp.arange(SEQ, dtype=jnp.int32)
    positions = order[index // half] * half + index % half
    base = jnp.log(positions.astype(jnp.float32) + 1.0) + 0.5
    noise_key = jax.random.fold_in(key, 23)
    noise = jax.random.uniform(noise_key, (BATCH, H, SEQ), jnp.float32, -1.0, 1.0)
    return base[None, None, :] + noise


def strengthened(values, key, source, target, blocks, factor):
    owner, partner = [(jnp.arange(values.shape[position]) // (values.shape[position] // blocks)).reshape([-1 if axis == position else 1 for axis in range(values.ndim)]) for position in (source, target)]
    chosen = jax.random.permutation(key, blocks)[partner]
    strong = (owner == chosen) | (owner == (partner + blocks // 2) % blocks)
    return jnp.where(strong, factor * values, values)


def block_levels(rng, shape, split, low, largest):
    def one(axis_at, shards_of):
        steps = jax.random.uniform(jax.random.fold_in(jax.random.fold_in(rng, 6), axis_at), (shards_of,), jnp.float32, low / len(split), largest / len(split))
        return jnp.repeat(jnp.exp(steps), shape[axis_at] // shards_of).reshape((-1,) + (1,) * (len(shape) - axis_at - 1))

    loudness = one(*split[0])
    for cut in split[1:]:
        loudness = loudness * one(*cut)
    return loudness


def gaussian(rng, dims, spread, bound, cuts=(), kind=jnp.bfloat16):
    result = jax.random.normal(rng, dims, jnp.float32) * spread
    if len(cuts) > 0:
        result = block_levels(rng, dims, cuts, -0.22, 0.18) * result
    return jnp.clip(result, min=-bound, max=bound).astype(kind)


def gaussian_with(stream_key, extent, deviation, limit, shards, heavy, kind=jnp.bfloat16):
    entries = deviation * jax.random.normal(stream_key, extent, jnp.float32)
    if shards:
        entries = entries * block_levels(stream_key, extent, shards, -0.22, 0.18)
    return jnp.clip(strengthened(entries, jax.random.fold_in(stream_key, 3), *heavy), -limit, limit).astype(kind)


def setup_inputs(seed: int = 0) -> dict:
    streams_of = jax.random.split(jax.random.key(seed), 9)
    return {
        "layer_input": gaussian_with(streams_of[0], (BATCH, SEQ, D), 0.01, 0.078125, ((0, 8), (1, 4)), (1, 2, 4, 2.0)),
        "query_rows": gaussian(streams_of[1], (BATCH, SEQ, H * DH), 1.0, 6.0, ((0, 8), (1, 4))),
        "key_rows": gaussian(streams_of[2], (BATCH, SEQ, DH), 1.0, 6.0, ((0, 8), (1, 4))),
        "value_rows": gaussian(streams_of[3], (BATCH, SEQ, DH), 1.0, 6.0, ((0, 8), (1, 4))),
        "attn_out": gaussian(streams_of[4], (BATCH, SEQ, H * DH), 1.0, 6.0, ((0, 8), (1, 4))),
        "d_attn": gaussian(streams_of[5], (BATCH, SEQ, H * DH), 1.0, 6.0, ((0, 8), (1, 4))),
        "log_sum_exp": draw_log_sum_exp(jax.random.fold_in(streams_of[8], 71), 0),
        "block_order": draw_block_order(jax.random.fold_in(streams_of[8], 71), 0),
    }


def reference(layer_input, query_rows, key_rows, value_rows, attn_out, d_attn, log_sum_exp, block_order):
    half = TOK_DEV // 2
    index = jnp.arange(SEQ, dtype=jnp.int32)
    positions = block_order[index // half].astype(jnp.int32) * half + index % half
    visible = positions[:, None] >= positions[None, :]
    scale = DH ** -0.5

    def single(item):
        q_seq, k_seq, v_seq, out_seq, grad_seq, stats = item
        queries = q_seq.reshape(SEQ, H, DH).astype(jnp.float32)
        grad_out = grad_seq.reshape(SEQ, H, DH).astype(jnp.float32)
        saved = out_seq.reshape(SEQ, H, DH).astype(jnp.float32)
        keys = k_seq.astype(jnp.float32)
        values = v_seq.astype(jnp.float32)
        delta = jnp.sum(grad_out * saved, axis=2).T
        score = jnp.einsum("rhd,sd->hrs", queries, keys) * scale
        prob = jnp.where(visible[None], jnp.exp(score - stats[:, :, None]), jnp.float32(0.0))
        prob_b = lax.optimization_barrier(prob.astype(jnp.bfloat16)).astype(jnp.float32)
        d_value = jnp.einsum("hrs,rhd->sd", prob_b, grad_out)
        d_prob = jnp.einsum("rhd,sd->hrs", grad_out, values)
        d_score = prob * (d_prob - delta[:, :, None])
        d_score = lax.optimization_barrier(d_score.astype(jnp.bfloat16)).astype(jnp.float32)
        d_query = jnp.einsum("hrs,sd->rhd", d_score, keys) * scale
        d_key = jnp.einsum("hrs,rhd->sd", d_score, queries) * scale
        d_kv = jnp.concatenate([d_key, d_value], axis=1).astype(jnp.bfloat16)
        return d_query.reshape(SEQ, H * DH).astype(jnp.bfloat16), d_kv

    d_query, d_kv = lax.map(single, (query_rows, key_rows, value_rows, attn_out, d_attn, log_sum_exp))
    flat_inputs = layer_input.reshape(BATCH * SEQ, D)
    flat_grads = d_kv.reshape(BATCH * SEQ, 2 * DH)
    d_weight = jnp.dot(flat_inputs.T, flat_grads, preferred_element_type=jnp.float32)
    return d_query, d_weight
```

```python
import jax
import jax.numpy as jnp
from jax import lax
from jax.experimental import pallas as pl
from jax.experimental.pallas import tpu as pltpu
from jax.sharding import PartitionSpec as P

MESH = pl.DeviceIdType.MESH
F32 = jnp.float32
BF16 = jnp.bfloat16
LOG2E = 1.4426950408889634
STRIPS = (2, 1, 3, 0)


def passed_along(value, axis, steps):
    count = lax.axis_size(axis)
    pairs = [(source, (source + steps) % count) for source in range(count)]
    return lax.ppermute(value, axis, pairs)


def slot_positions(block_order, owner, half):
    firsts = lax.dynamic_slice_in_dim(block_order, 2 * owner, 2)
    offsets = jnp.arange(half, dtype=jnp.int32)
    return (firsts[:, None] * half + offsets[None, :]).reshape(2 * half)


def body(layer_input, query_rows, key_rows, value_rows, attn_out, d_attn, log_sum_exp, block_order):
    rows = query_rows.shape[1]
    head_dim = key_rows.shape[2]
    heads = query_rows.shape[2] // head_dim
    half = rows // 2
    scale = head_dim ** (-0.5)
    width = lax.axis_size("ctx")
    mine = lax.axis_index("ctx")
    q_pos = slot_positions(block_order, mine, half)
    queries = query_rows[0].reshape(rows, heads, head_dim)
    grad_out = d_attn[0].reshape(rows, heads, head_dim)
    saved = attn_out[0].reshape(rows, heads, head_dim)
    delta = jnp.sum(grad_out.astype(jnp.float32) * saved.astype(jnp.float32), axis=2).T
    stats = log_sum_exp[0]

    def tile(pair, k_pos):
        keys = pair[0]
        values = pair[1]
        score = jnp.einsum("rhd,sd->hrs", queries, keys, preferred_element_type=jnp.float32) * scale
        visible = q_pos[:, None] >= k_pos[None, :]
        prob = jnp.where(visible[None], jnp.exp(score - stats[:, :, None]), 0.0)
        d_value = jnp.einsum(
            "hrs,rhd->sd", prob.astype(jnp.bfloat16), grad_out, preferred_element_type=jnp.float32
        )
        d_prob = jnp.einsum("rhd,sd->hrs", grad_out, values, preferred_element_type=jnp.float32)
        d_score = (prob * (d_prob - delta[:, :, None])).astype(jnp.bfloat16)
        d_query = (
            jnp.einsum("hrs,sd->rhd", d_score, keys, preferred_element_type=jnp.float32) * scale
        )
        d_key = (
            jnp.einsum("hrs,rhd->sd", d_score, queries, preferred_element_type=jnp.float32) * scale
        )
        return (d_query, jnp.stack([d_key, d_value]))

    pair = jnp.stack([key_rows[0], value_rows[0]])
    query_zero = jnp.zeros((rows, heads, head_dim), jnp.float32)

    def pass_grads(sums):
        return passed_along(sums, "ctx", 1)

    def cycle_step(step, carry):
        pair_now, sums, query_sum = carry
        owner = (mine - step) % width
        d_query, d_kv = tile(pair_now, slot_positions(block_order, owner, half))
        sums = pass_grads(sums + d_kv)
        pair_now = passed_along(pair_now, "ctx", 1)
        return (pair_now, sums, query_sum + d_query)

    start = (pair, jnp.zeros((2, rows, head_dim), jnp.float32), query_zero)
    pair_last, sums, query_sum = lax.fori_loop(0, width - 1, cycle_step, start)
    d_query, d_kv = tile(pair_last, slot_positions(block_order, (mine + 1) % width, half))
    kv_sums = pass_grads(sums + d_kv)
    query_sum = query_sum + d_query
    d_query_out = query_sum.reshape(1, rows, heads * head_dim).astype(jnp.bfloat16)
    grads_bf = jnp.concatenate([kv_sums[0], kv_sums[1]], axis=1).astype(jnp.bfloat16)
    inputs = layer_input[0]
    d_weight = lax.psum_scatter(
        lax.dot_general(
            inputs, grads_bf, (((0,), (0,)), ((), ())), preferred_element_type=jnp.float32
        ),
        ("dp", "ctx"),
        scatter_dimension=0,
        tiled=True,
    )
    return (d_query_out, d_weight)


def dot(left, right, contract=((1,), (0,))):
    return lax.dot_general(left, right, (contract, ((), ())), preferred_element_type=F32)


def fused_kernel(
    x_ref, q_ref, k_ref, v_ref, o_ref, do_ref, lse_ref, order_ref,
    dq_ref, dw_ref,
    xbuf, kv, lse2, delta, dq_acc, own, acc, g_send, g_recv, g_mine, g_other,
    a_keep, b_keep, a1_send, a1_recv, b1_send, b1_recv,
    a2_send, a2_recv, b2_send, b2_recv, last_keep, last_send, last_recv,
    x_local, x_send, x_recv, kv_ssem, kv_rsem, g_ssem, g_rsem,
    a1_ssem, a1_rsem, b1_ssem, b1_rsem, a2_ssem, a2_rsem, b2_ssem, b2_rsem,
    last_ssem, last_rsem,
):
    rows, dh = k_ref.shape[1], k_ref.shape[2]
    heads = q_ref.shape[2] // dh
    half = rows // 2
    scale = dh ** (-0.5)
    dp, ctx = lax.axis_index("dp"), lax.axis_index("ctx")
    z, y = dp // 2, dp % 2
    x, c = ctx // 2, ctx % 2
    mate = (dp, 2 * x + 1 - c)
    side = (dp, 2 * (1 - x) + c)
    cross = (dp, 2 * (1 - x) + 1 - c)
    over = (2 * z + 1 - y, ctx)
    along = [(2 * ((z + k) % 4) + y, ctx) for k in (1, 2, 3)]

    barrier = pltpu.get_barrier_semaphore()
    everyone = [mate, side, cross, over] + along
    for peer in everyone:
        pl.semaphore_signal(barrier, inc=1, device_id=peer, device_id_type=MESH)
    kv[0, :, 0:dh] = k_ref[0]
    kv[0, :, dh : 2 * dh] = v_ref[0]
    pl.semaphore_wait(barrier, len(everyone))

    started = []

    def send(source, target, ssem, rsem, peer):
        copy = pltpu.make_async_remote_copy(
            src_ref=source, dst_ref=target, send_sem=ssem, recv_sem=rsem,
            device_id=peer, device_id_type=MESH,
        )
        copy.start()
        started.append(copy)
        return copy

    kv_side = send(kv.at[0], kv.at[1], kv_ssem.at[0], kv_rsem.at[0], side)
    kv_mate = send(kv.at[0], kv.at[3], kv_ssem.at[2], kv_rsem.at[2], mate)

    def x_copies(m):
        mine = pl.ds(pl.multiple_of((2 * m + c) * rows, rows), rows)
        theirs = pl.ds(pl.multiple_of((2 * m + 1 - c) * rows, rows), rows)
        here = pltpu.make_async_copy(
            x_ref.at[0, :, mine], xbuf.at[m, pl.ds(0, rows), :], x_local.at[m]
        )
        there = pltpu.make_async_remote_copy(
            src_ref=x_ref.at[0, :, theirs], dst_ref=xbuf.at[m, pl.ds(rows, rows), :],
            send_sem=x_send.at[m], recv_sem=x_recv.at[m], device_id=mate, device_id_type=MESH,
        )
        return here, there

    @pl.loop(0, 16)
    def _(m):
        here, there = x_copies(m)
        there.start()
        here.start()

    lse2[...] = lse_ref[0] * LOG2E

    @pl.loop(0, heads)
    def _(h):
        cols = pl.ds(pl.multiple_of(h * dh, dh), dh)
        product = do_ref[0, :, cols].astype(F32) * o_ref[0, :, cols].astype(F32)
        delta[pl.ds(h, 1), :] = jnp.sum(product.T, axis=0, keepdims=True)

    ahead = lax.broadcasted_iota(jnp.int32, (half, half), 1) - lax.broadcasted_iota(
        jnp.int32, (half, half), 0
    )

    def chunk(slot, owner, total, first):
        keys = kv[slot, :, 0:dh]
        values = kv[slot, :, dh : 2 * dh]
        keys_t = keys.astype(F32).T.astype(BF16)
        total[...] = jnp.zeros_like(total)

        def visible():
            return jnp.concatenate(
                [
                    jnp.concatenate(
                        [
                            ahead >= (order_ref[2 * owner + a] - order_ref[2 * ctx + b]) * half
                            for b in range(2)
                        ],
                        axis=1,
                    )
                    for a in range(2)
                ],
                axis=0,
            )

        def one(h):
            cols = pl.ds(pl.multiple_of(h * dh, dh), dh)
            query = q_ref[0, :, cols]
            grad = do_ref[0, :, cols]
            score = dot(keys, query, ((1,), (1,)))
            d_prob = dot(values, grad, ((1,), (1,)))
            prob = jnp.where(
                visible(), jnp.exp2(score * (scale * LOG2E) - lse2[pl.ds(h, 1), :]), 0.0
            )
            prob_b = prob.astype(BF16)
            d_score = (prob * (d_prob - delta[pl.ds(h, 1), :])).astype(BF16)
            d_value = dot(prob_b, grad)
            d_key = dot(d_score, query)
            d_query = dot(keys_t, d_score)
            if first:
                dq_acc[h] = d_query
            else:
                dq_acc[h] += d_query
            return d_key, d_value

        @pl.loop(0, heads // 2)
        def _(pair):
            key_a, value_a = one(2 * pair)
            key_b, value_b = one(2 * pair + 1)
            total[:, 0:dh] += key_a + key_b
            total[:, dh : 2 * dh] += value_a + value_b

    def give(slot, peer):
        g_send[slot - 1, :, 0:dh] = (acc[:, 0:dh] * scale).astype(BF16)
        g_send[slot - 1, :, dh : 2 * dh] = acc[:, dh : 2 * dh].astype(BF16)
        return send(
            g_send.at[slot - 1], g_recv.at[slot - 1], g_ssem.at[slot - 1], g_rsem.at[slot - 1], peer
        )

    chunk(0, ctx, own, True)
    kv_side.wait_recv()
    kv_cross = send(kv.at[1], kv.at[2], kv_ssem.at[1], kv_rsem.at[1], mate)
    chunk(1, side[1], acc, False)
    given = [give(1, side)]
    kv_cross.wait_recv()
    chunk(2, cross[1], acc, False)
    given.append(give(2, cross))
    kv_mate.wait_recv()
    chunk(3, mate[1], acc, False)
    given.append(give(3, mate))

    @pl.loop(0, heads)
    def _(h):
        cols = pl.ds(pl.multiple_of(h * dh, dh), dh)
        dq_ref[0, :, cols] = (dq_acc[h] * scale).T.astype(BF16)

    for copy in given:
        copy.wait_recv()
    d_key = own[:, 0:dh] * scale
    d_value = own[:, dh : 2 * dh]
    for slot in range(3):
        d_key = d_key + g_recv[slot, :, 0:dh].astype(F32)
        d_value = d_value + g_recv[slot, :, dh : 2 * dh].astype(F32)
    g_mine[0:dh, :] = d_key.T.astype(BF16)
    g_mine[dh : 2 * dh, :] = d_value.T.astype(BF16)
    g_copy = send(g_mine, g_other, g_ssem.at[3], g_rsem.at[3], mate)

    @pl.loop(0, 16)
    def _(m):
        here, there = x_copies(m)
        here.wait()
        there.wait()

    g_copy.wait_recv()

    first_a, first_b, second_a, second_b, final = {}, {}, {}, {}, {}

    def stage_one(k):
        strip = (z + k) % 4
        for yr in range(2):
            for xr in range(2):
                m = strip * 4 + (y + yr) % 2 * 2 + (x + xr) % 2
                part = dot(g_mine[...], xbuf[m, 0:rows, :]) + dot(
                    g_other[...], xbuf[m, rows : 2 * rows, :]
                )
                if xr:
                    a1_send[k, yr] = part[0:dh].astype(BF16)
                else:
                    a_keep[k, yr] = part[0:dh]
                if yr:
                    b1_send[k, xr] = part[dh : 2 * dh].astype(BF16)
                else:
                    b_keep[k, xr] = part[dh : 2 * dh]
        first_a[k] = send(a1_send.at[k], a1_recv.at[k], a1_ssem.at[k], a1_rsem.at[k], side)
        first_b[k] = send(b1_send.at[k], b1_recv.at[k], b1_ssem.at[k], b1_rsem.at[k], over)

    def stage_two(k):
        first_a[k].wait_recv()
        a2_send[k] = (a_keep[k, 1] + a1_recv[k, 1].astype(F32)).astype(BF16)
        second_a[k] = send(a2_send.at[k], a2_recv.at[k], a2_ssem.at[k], a2_rsem.at[k], over)
        first_b[k].wait_recv()
        b2_send[k] = (b_keep[k, 1] + b1_recv[k, 1].astype(F32)).astype(BF16)
        second_b[k] = send(b2_send.at[k], b2_recv.at[k], b2_ssem.at[k], b2_rsem.at[k], side)

    def stage_three(k):
        second_a[k].wait_recv()
        second_b[k].wait_recv()
        sum_a = a_keep[k, 0] + a1_recv[k, 0].astype(F32) + a2_recv[k].astype(F32)
        sum_b = b_keep[k, 0] + b1_recv[k, 0].astype(F32) + b2_recv[k].astype(F32)
        if k:
            last_send[k - 1, 0:dh, :] = sum_a.astype(BF16)
            last_send[k - 1, dh : 2 * dh, :] = sum_b.astype(BF16)
            final[k] = send(
                last_send.at[k - 1], last_recv.at[k - 1],
                last_ssem.at[k - 1], last_rsem.at[k - 1], along[k - 1],
            )
        else:
            last_keep[0:dh, :] = sum_a
            last_keep[dh : 2 * dh, :] = sum_b

    s = STRIPS
    stage_one(s[0])
    stage_one(s[1])
    stage_two(s[0])
    stage_one(s[2])
    stage_two(s[1])
    stage_three(s[0])
    stage_one(s[3])
    stage_two(s[2])
    stage_three(s[1])
    stage_two(s[3])
    stage_three(s[2])
    stage_three(s[3])
    for k in (1, 2, 3):
        final[k].wait_recv()
    result = last_keep[...]
    for k in range(3):
        result = result + last_recv[k].astype(F32)
    dw_ref[...] = result.T
    for copy in started:
        copy.wait_send()


def fused_body(layer_input, query_rows, key_rows, value_rows, attn_out, d_attn, log_sum_exp, block_order):
    rows, dh = key_rows.shape[1], key_rows.shape[2]
    heads = query_rows.shape[2] // dh
    wide = 2 * dh
    vmem = pl.BlockSpec(memory_space=pltpu.VMEM)
    dma = pltpu.SemaphoreType.DMA
    return pl.pallas_call(
        fused_kernel,
        out_shape=(
            jax.ShapeDtypeStruct(query_rows.shape, BF16),
            jax.ShapeDtypeStruct((rows, wide), F32),
        ),
        in_specs=[pl.BlockSpec(memory_space=pl.ANY)] + [vmem] * 6 + [pl.BlockSpec(memory_space=pltpu.SMEM)],
        out_specs=(vmem, vmem),
        scratch_shapes=[
            pltpu.VMEM((16, 2 * rows, rows), BF16),
            pltpu.VMEM((4, rows, wide), BF16),
            pltpu.VMEM((heads, rows), F32),
            pltpu.VMEM((heads, rows), F32),
            pltpu.VMEM((heads, dh, rows), F32),
            pltpu.VMEM((rows, wide), F32),
            pltpu.VMEM((rows, wide), F32),
            pltpu.VMEM((3, rows, wide), BF16),
            pltpu.VMEM((3, rows, wide), BF16),
            pltpu.VMEM((wide, rows), BF16),
            pltpu.VMEM((wide, rows), BF16),
            pltpu.VMEM((4, 2, dh, rows), F32),
            pltpu.VMEM((4, 2, dh, rows), F32),
            pltpu.VMEM((4, 2, dh, rows), BF16),
            pltpu.VMEM((4, 2, dh, rows), BF16),
            pltpu.VMEM((4, 2, dh, rows), BF16),
            pltpu.VMEM((4, 2, dh, rows), BF16),
            pltpu.VMEM((4, dh, rows), BF16),
            pltpu.VMEM((4, dh, rows), BF16),
            pltpu.VMEM((4, dh, rows), BF16),
            pltpu.VMEM((4, dh, rows), BF16),
            pltpu.VMEM((wide, rows), F32),
            pltpu.VMEM((3, wide, rows), BF16),
            pltpu.VMEM((3, wide, rows), BF16),
            dma((16,)), dma((16,)), dma((16,)),
            dma((3,)), dma((3,)), dma((4,)), dma((4,)),
            dma((4,)), dma((4,)), dma((4,)), dma((4,)),
            dma((4,)), dma((4,)), dma((4,)), dma((4,)),
            dma((3,)), dma((3,)),
        ],
        compiler_params=pltpu.CompilerParams(
            collective_id=0, has_side_effects=True, vmem_limit_bytes=40 * 1024 * 1024
        ),
        cost_estimate=pl.CostEstimate(
            flops=4 * 10 * heads * rows * rows * dh + 4 * rows * rows * wide * 16,
            bytes_accessed=8 * 1024 * 1024,
            transcendentals=4 * heads * rows * rows,
        ),
    )(layer_input, query_rows, key_rows, value_rows, attn_out, d_attn, log_sum_exp, block_order)


def fits(mesh):
    return dict(mesh.shape) == {"dp": 8, "ctx": 4}


def solution(mesh):
    return jax.shard_map(
        fused_body if fits(mesh) else body,
        mesh=mesh,
        in_specs=(
            P("dp", "ctx", None),
            P("dp", "ctx", None),
            P("dp", "ctx", None),
            P("dp", "ctx", None),
            P("dp", "ctx", None),
            P("dp", "ctx", None),
            P("dp", None, "ctx"),
            P(),
        ),
        out_specs=(P("dp", "ctx", None), P(("dp", "ctx"), None)),
        check_vma=False,
    )
```

```python
import jax
import jax.numpy as jnp
from jax import lax
from jax.experimental import pallas as pl
from jax.experimental.pallas import tpu as pltpu
from jax.sharding import PartitionSpec as P

MESH = pl.DeviceIdType.MESH
F32 = jnp.float32
BF16 = jnp.bfloat16
LOG2E = 1.4426950408889634
STRIPS = (2, 1, 3, 0)


def passed_along(value, axis, steps):
    count = lax.axis_size(axis)
    pairs = [(source, (source + steps) % count) for source in range(count)]
    return lax.ppermute(value, axis, pairs)


def slot_positions(block_order, owner, half):
    firsts = lax.dynamic_slice_in_dim(block_order, 2 * owner, 2)
    offsets = jnp.arange(half, dtype=jnp.int32)
    return (firsts[:, None] * half + offsets[None, :]).reshape(2 * half)


def body(layer_input, query_rows, key_rows, value_rows, attn_out, d_attn, log_sum_exp, block_order):
    rows = query_rows.shape[1]
    head_dim = key_rows.shape[2]
    heads = query_rows.shape[2] // head_dim
    half = rows // 2
    scale = head_dim ** (-0.5)
    width = lax.axis_size("ctx")
    mine = lax.axis_index("ctx")
    q_pos = slot_positions(block_order, mine, half)
    queries = query_rows[0].reshape(rows, heads, head_dim)
    grad_out = d_attn[0].reshape(rows, heads, head_dim)
    saved = attn_out[0].reshape(rows, heads, head_dim)
    delta = jnp.sum(grad_out.astype(jnp.float32) * saved.astype(jnp.float32), axis=2).T
    stats = log_sum_exp[0]

    def tile(pair, k_pos):
        keys = pair[0]
        values = pair[1]
        score = jnp.einsum("rhd,sd->hrs", queries, keys, preferred_element_type=jnp.float32) * scale
        visible = q_pos[:, None] >= k_pos[None, :]
        prob = jnp.where(visible[None], jnp.exp(score - stats[:, :, None]), 0.0)
        d_value = jnp.einsum(
            "hrs,rhd->sd", prob.astype(jnp.bfloat16), grad_out, preferred_element_type=jnp.float32
        )
        d_prob = jnp.einsum("rhd,sd->hrs", grad_out, values, preferred_element_type=jnp.float32)
        d_score = (prob * (d_prob - delta[:, :, None])).astype(jnp.bfloat16)
        d_query = (
            jnp.einsum("hrs,sd->rhd", d_score, keys, preferred_element_type=jnp.float32) * scale
        )
        d_key = (
            jnp.einsum("hrs,rhd->sd", d_score, queries, preferred_element_type=jnp.float32) * scale
        )
        return (d_query, jnp.stack([d_key, d_value]))

    pair = jnp.stack([key_rows[0], value_rows[0]])
    query_zero = jnp.zeros((rows, heads, head_dim), jnp.float32)

    def pass_grads(sums):
        return passed_along(sums, "ctx", 1)

    def cycle_step(step, carry):
        pair_now, sums, query_sum = carry
        owner = (mine - step) % width
        d_query, d_kv = tile(pair_now, slot_positions(block_order, owner, half))
        sums = pass_grads(sums + d_kv)
        pair_now = passed_along(pair_now, "ctx", 1)
        return (pair_now, sums, query_sum + d_query)

    start = (pair, jnp.zeros((2, rows, head_dim), jnp.float32), query_zero)
    pair_last, sums, query_sum = lax.fori_loop(0, width - 1, cycle_step, start)
    d_query, d_kv = tile(pair_last, slot_positions(block_order, (mine + 1) % width, half))
    kv_sums = pass_grads(sums + d_kv)
    query_sum = query_sum + d_query
    d_query_out = query_sum.reshape(1, rows, heads * head_dim).astype(jnp.bfloat16)
    grads_bf = jnp.concatenate([kv_sums[0], kv_sums[1]], axis=1).astype(jnp.bfloat16)
    inputs = layer_input[0]
    d_weight = lax.psum_scatter(
        lax.dot_general(
            inputs, grads_bf, (((0,), (0,)), ((), ())), preferred_element_type=jnp.float32
        ),
        ("dp", "ctx"),
        scatter_dimension=0,
        tiled=True,
    )
    return (d_query_out, d_weight)


def dot(left, right, contract=((1,), (0,))):
    return lax.dot_general(left, right, (contract, ((), ())), preferred_element_type=F32)


def fused_kernel(
    x_ref, q_hbm, k_hbm, v_hbm, o_hbm, do_hbm, lse_hbm, order_ref,
    dq_ref, dw_ref,
    q_ref, o_ref, do_ref, lse_ref, xbuf, kv, lse2, delta, dq_acc, own, acc, g_send, g_recv, g_mine, g_other,
    a_keep, b_keep, a1_send, a1_recv, b1_send, b1_recv,
    a2_send, a2_recv, b2_send, b2_recv, last_keep, last_send, last_recv,
    x_local, x_send, x_recv, kv_ssem, kv_rsem, g_ssem, g_rsem,
    a1_ssem, a1_rsem, b1_ssem, b1_rsem, a2_ssem, a2_rsem, b2_ssem, b2_rsem,
    last_ssem, last_rsem, in_sem,
):
    rows, dh = k_hbm.shape[1], k_hbm.shape[2]
    heads = q_ref.shape[2] // dh
    half = rows // 2
    scale = dh ** (-0.5)
    dp, ctx = lax.axis_index("dp"), lax.axis_index("ctx")
    z, y = dp // 2, dp % 2
    x, c = ctx // 2, ctx % 2
    mate = (dp, 2 * x + 1 - c)
    side = (dp, 2 * (1 - x) + c)
    cross = (dp, 2 * (1 - x) + 1 - c)
    over = (2 * z + 1 - y, ctx)
    along = [(2 * ((z + k) % 4) + y, ctx) for k in (1, 2, 3)]

    loads = [
        pltpu.make_async_copy(source, target, in_sem.at[i])
        for i, (source, target) in enumerate(
            (
                (k_hbm.at[0], kv.at[0, :, pl.ds(0, dh)]),
                (v_hbm.at[0], kv.at[0, :, pl.ds(dh, dh)]),
                (do_hbm, do_ref),
                (o_hbm, o_ref),
                (q_hbm, q_ref),
                (lse_hbm, lse_ref),
            )
        )
    ]
    for copy in loads:
        copy.start()

    barrier = pltpu.get_barrier_semaphore()
    everyone = [mate, side, cross, over] + along
    for peer in everyone:
        pl.semaphore_signal(barrier, inc=1, device_id=peer, device_id_type=MESH)
    pl.semaphore_wait(barrier, len(everyone))
    loads[0].wait()
    loads[1].wait()

    started = []

    def send(source, target, ssem, rsem, peer):
        copy = pltpu.make_async_remote_copy(
            src_ref=source, dst_ref=target, send_sem=ssem, recv_sem=rsem,
            device_id=peer, device_id_type=MESH,
        )
        copy.start()
        started.append(copy)
        return copy

    kv_side = send(kv.at[0], kv.at[1], kv_ssem.at[0], kv_rsem.at[0], side)
    kv_mate = send(kv.at[0], kv.at[3], kv_ssem.at[2], kv_rsem.at[2], mate)

    def x_copies(m):
        mine = pl.ds(pl.multiple_of((2 * m + c) * rows, rows), rows)
        theirs = pl.ds(pl.multiple_of((2 * m + 1 - c) * rows, rows), rows)
        here = pltpu.make_async_copy(
            x_ref.at[0, :, mine], xbuf.at[m, pl.ds(0, rows), :], x_local.at[m]
        )
        there = pltpu.make_async_remote_copy(
            src_ref=x_ref.at[0, :, theirs], dst_ref=xbuf.at[m, pl.ds(rows, rows), :],
            send_sem=x_send.at[m], recv_sem=x_recv.at[m], device_id=mate, device_id_type=MESH,
        )
        return here, there

    @pl.loop(0, 16)
    def _(m):
        here, there = x_copies(m)
        there.start()
        here.start()

    for copy in loads[2:]:
        copy.wait()
    lse2[...] = lse_ref[0] * LOG2E

    @pl.loop(0, heads)
    def _(h):
        cols = pl.ds(pl.multiple_of(h * dh, dh), dh)
        product = do_ref[0, :, cols].astype(F32) * o_ref[0, :, cols].astype(F32)
        delta[pl.ds(h, 1), :] = jnp.sum(product.T, axis=0, keepdims=True)

    ahead = lax.broadcasted_iota(jnp.int32, (half, half), 1) - lax.broadcasted_iota(
        jnp.int32, (half, half), 0
    )

    def chunk(slot, owner, total, first):
        keys = kv[slot, :, 0:dh]
        values = kv[slot, :, dh : 2 * dh]
        keys_t = keys.astype(F32).T.astype(BF16)
        total[...] = jnp.zeros_like(total)

        def visible():
            return jnp.concatenate(
                [
                    jnp.concatenate(
                        [
                            ahead >= (order_ref[2 * owner + a] - order_ref[2 * ctx + b]) * half
                            for b in range(2)
                        ],
                        axis=1,
                    )
                    for a in range(2)
                ],
                axis=0,
            )

        def one(h):
            cols = pl.ds(pl.multiple_of(h * dh, dh), dh)
            query = q_ref[0, :, cols]
            grad = do_ref[0, :, cols]
            score = dot(keys, query, ((1,), (1,)))
            d_prob = dot(values, grad, ((1,), (1,)))
            prob = jnp.where(
                visible(), jnp.exp2(score * (scale * LOG2E) - lse2[pl.ds(h, 1), :]), 0.0
            )
            prob_b = prob.astype(BF16)
            d_score = (prob * (d_prob - delta[pl.ds(h, 1), :])).astype(BF16)
            d_value = dot(prob_b, grad)
            d_key = dot(d_score, query)
            d_query = dot(keys_t, d_score)
            if first:
                dq_acc[h] = d_query
            else:
                dq_acc[h] += d_query
            return d_key, d_value

        @pl.loop(0, heads // 4)
        def _(group):
            parts = [one(4 * group + i) for i in range(4)]
            total[:, 0:dh] += (parts[0][0] + parts[1][0]) + (parts[2][0] + parts[3][0])
            total[:, dh : 2 * dh] += (parts[0][1] + parts[1][1]) + (parts[2][1] + parts[3][1])

    def give(slot, peer):
        g_send[slot - 1, :, 0:dh] = (acc[:, 0:dh] * scale).astype(BF16)
        g_send[slot - 1, :, dh : 2 * dh] = acc[:, dh : 2 * dh].astype(BF16)
        return send(
            g_send.at[slot - 1], g_recv.at[slot - 1], g_ssem.at[slot - 1], g_rsem.at[slot - 1], peer
        )

    chunk(0, ctx, own, True)
    kv_side.wait_recv()
    kv_cross = send(kv.at[1], kv.at[2], kv_ssem.at[1], kv_rsem.at[1], mate)
    chunk(1, side[1], acc, False)
    given = [give(1, side)]
    kv_cross.wait_recv()
    chunk(2, cross[1], acc, False)
    given.append(give(2, cross))
    kv_mate.wait_recv()
    chunk(3, mate[1], acc, False)
    given.append(give(3, mate))

    @pl.loop(0, heads)
    def _(h):
        cols = pl.ds(pl.multiple_of(h * dh, dh), dh)
        dq_ref[0, :, cols] = (dq_acc[h] * scale).T.astype(BF16)

    for copy in given:
        copy.wait_recv()
    d_key = own[:, 0:dh] * scale
    d_value = own[:, dh : 2 * dh]
    for slot in range(3):
        d_key = d_key + g_recv[slot, :, 0:dh].astype(F32)
        d_value = d_value + g_recv[slot, :, dh : 2 * dh].astype(F32)
    g_mine[0:dh, :] = d_key.T.astype(BF16)
    g_mine[dh : 2 * dh, :] = d_value.T.astype(BF16)
    g_copy = send(g_mine, g_other, g_ssem.at[3], g_rsem.at[3], mate)

    @pl.loop(0, 16)
    def _(m):
        here, there = x_copies(m)
        here.wait()
        there.wait()

    g_copy.wait_recv()

    first_a, first_b, second_a, second_b, final = {}, {}, {}, {}, {}

    def stage_one(k):
        strip = (z + k) % 4
        for yr in range(2):
            for xr in range(2):
                m = strip * 4 + (y + yr) % 2 * 2 + (x + xr) % 2
                part = dot(g_mine[...], xbuf[m, 0:rows, :]) + dot(
                    g_other[...], xbuf[m, rows : 2 * rows, :]
                )
                if xr:
                    a1_send[k, yr] = part[0:dh].astype(BF16)
                else:
                    a_keep[k, yr] = part[0:dh]
                if yr:
                    b1_send[k, xr] = part[dh : 2 * dh].astype(BF16)
                else:
                    b_keep[k, xr] = part[dh : 2 * dh]
        first_a[k] = send(a1_send.at[k], a1_recv.at[k], a1_ssem.at[k], a1_rsem.at[k], side)
        first_b[k] = send(b1_send.at[k], b1_recv.at[k], b1_ssem.at[k], b1_rsem.at[k], over)

    def stage_two(k):
        first_a[k].wait_recv()
        a2_send[k] = (a_keep[k, 1] + a1_recv[k, 1].astype(F32)).astype(BF16)
        second_a[k] = send(a2_send.at[k], a2_recv.at[k], a2_ssem.at[k], a2_rsem.at[k], over)
        first_b[k].wait_recv()
        b2_send[k] = (b_keep[k, 1] + b1_recv[k, 1].astype(F32)).astype(BF16)
        second_b[k] = send(b2_send.at[k], b2_recv.at[k], b2_ssem.at[k], b2_rsem.at[k], side)

    def stage_three(k):
        second_a[k].wait_recv()
        second_b[k].wait_recv()
        sum_a = a_keep[k, 0] + a1_recv[k, 0].astype(F32) + a2_recv[k].astype(F32)
        sum_b = b_keep[k, 0] + b1_recv[k, 0].astype(F32) + b2_recv[k].astype(F32)
        if k:
            last_send[k - 1, 0:dh, :] = sum_a.astype(BF16)
            last_send[k - 1, dh : 2 * dh, :] = sum_b.astype(BF16)
            final[k] = send(
                last_send.at[k - 1], last_recv.at[k - 1],
                last_ssem.at[k - 1], last_rsem.at[k - 1], along[k - 1],
            )
        else:
            last_keep[0:dh, :] = sum_a
            last_keep[dh : 2 * dh, :] = sum_b

    s = STRIPS
    stage_one(s[0])
    stage_one(s[1])
    stage_two(s[0])
    stage_one(s[2])
    stage_two(s[1])
    stage_three(s[0])
    stage_one(s[3])
    stage_two(s[2])
    stage_three(s[1])
    stage_two(s[3])
    stage_three(s[2])
    stage_three(s[3])
    for k in (1, 2, 3):
        final[k].wait_recv()
    result = last_keep[...]
    for k in range(3):
        result = result + last_recv[k].astype(F32)
    dw_ref[...] = result.T
    for copy in started:
        copy.wait_send()


def fused_body(layer_input, query_rows, key_rows, value_rows, attn_out, d_attn, log_sum_exp, block_order):
    rows, dh = key_rows.shape[1], key_rows.shape[2]
    heads = query_rows.shape[2] // dh
    wide = 2 * dh
    vmem = pl.BlockSpec(memory_space=pltpu.VMEM)
    dma = pltpu.SemaphoreType.DMA
    return pl.pallas_call(
        fused_kernel,
        out_shape=(
            jax.ShapeDtypeStruct(query_rows.shape, BF16),
            jax.ShapeDtypeStruct((rows, wide), F32),
        ),
        in_specs=[pl.BlockSpec(memory_space=pltpu.HBM)] * 7 + [pl.BlockSpec(memory_space=pltpu.SMEM)],
        out_specs=(vmem, vmem),
        scratch_shapes=[
            pltpu.VMEM(query_rows.shape, BF16),
            pltpu.VMEM(query_rows.shape, BF16),
            pltpu.VMEM(query_rows.shape, BF16),
            pltpu.VMEM(log_sum_exp.shape, F32),
            pltpu.VMEM((16, 2 * rows, rows), BF16),
            pltpu.VMEM((4, rows, wide), BF16),
            pltpu.VMEM((heads, rows), F32),
            pltpu.VMEM((heads, rows), F32),
            pltpu.VMEM((heads, dh, rows), F32),
            pltpu.VMEM((rows, wide), F32),
            pltpu.VMEM((rows, wide), F32),
            pltpu.VMEM((3, rows, wide), BF16),
            pltpu.VMEM((3, rows, wide), BF16),
            pltpu.VMEM((wide, rows), BF16),
            pltpu.VMEM((wide, rows), BF16),
            pltpu.VMEM((4, 2, dh, rows), F32),
            pltpu.VMEM((4, 2, dh, rows), F32),
            pltpu.VMEM((4, 2, dh, rows), BF16),
            pltpu.VMEM((4, 2, dh, rows), BF16),
            pltpu.VMEM((4, 2, dh, rows), BF16),
            pltpu.VMEM((4, 2, dh, rows), BF16),
            pltpu.VMEM((4, dh, rows), BF16),
            pltpu.VMEM((4, dh, rows), BF16),
            pltpu.VMEM((4, dh, rows), BF16),
            pltpu.VMEM((4, dh, rows), BF16),
            pltpu.VMEM((wide, rows), F32),
            pltpu.VMEM((3, wide, rows), BF16),
            pltpu.VMEM((3, wide, rows), BF16),
            dma((16,)), dma((16,)), dma((16,)),
            dma((3,)), dma((3,)), dma((4,)), dma((4,)),
            dma((4,)), dma((4,)), dma((4,)), dma((4,)),
            dma((4,)), dma((4,)), dma((4,)), dma((4,)),
            dma((3,)), dma((3,)), dma((6,)),
        ],
        compiler_params=pltpu.CompilerParams(
            collective_id=0, has_side_effects=True, vmem_limit_bytes=64 * 1024 * 1024
        ),
        cost_estimate=pl.CostEstimate(
            flops=4 * 10 * heads * rows * rows * dh + 4 * rows * rows * wide * 16,
            bytes_accessed=8 * 1024 * 1024,
            transcendentals=4 * heads * rows * rows,
        ),
    )(layer_input, query_rows, key_rows, value_rows, attn_out, d_attn, log_sum_exp, block_order)


def fits(mesh):
    return dict(mesh.shape) == {"dp": 8, "ctx": 4}


def solution(mesh):
    return jax.shard_map(
        fused_body if fits(mesh) else body,
        mesh=mesh,
        in_specs=(
            P("dp", "ctx", None),
            P("dp", "ctx", None),
            P("dp", "ctx", None),
            P("dp", "ctx", None),
            P("dp", "ctx", None),
            P("dp", "ctx", None),
            P("dp", None, "ctx"),
            P(),
        ),
        out_specs=(P("dp", "ctx", None), P(("dp", "ctx"), None)),
        check_vma=False,
    )
```

```python
import jax
import jax.numpy as jnp
from jax import lax
from jax.experimental import pallas as pl
from jax.experimental.pallas import tpu as pltpu
from jax.sharding import PartitionSpec as P

MESH = pl.DeviceIdType.MESH
F32 = jnp.float32
BF16 = jnp.bfloat16
LOG2E = 1.4426950408889634
STRIPS = (2, 1, 3, 0)


def passed_along(value, axis, steps):
    count = lax.axis_size(axis)
    pairs = [(source, (source + steps) % count) for source in range(count)]
    return lax.ppermute(value, axis, pairs)


def slot_positions(block_order, owner, half):
    firsts = lax.dynamic_slice_in_dim(block_order, 2 * owner, 2)
    offsets = jnp.arange(half, dtype=jnp.int32)
    return (firsts[:, None] * half + offsets[None, :]).reshape(2 * half)


def body(layer_input, query_rows, key_rows, value_rows, attn_out, d_attn, log_sum_exp, block_order):
    rows = query_rows.shape[1]
    head_dim = key_rows.shape[2]
    heads = query_rows.shape[2] // head_dim
    half = rows // 2
    scale = head_dim ** (-0.5)
    width = lax.axis_size("ctx")
    mine = lax.axis_index("ctx")
    q_pos = slot_positions(block_order, mine, half)
    queries = query_rows[0].reshape(rows, heads, head_dim)
    grad_out = d_attn[0].reshape(rows, heads, head_dim)
    saved = attn_out[0].reshape(rows, heads, head_dim)
    delta = jnp.sum(grad_out.astype(jnp.float32) * saved.astype(jnp.float32), axis=2).T
    stats = log_sum_exp[0]

    def tile(pair, k_pos):
        keys = pair[0]
        values = pair[1]
        score = jnp.einsum("rhd,sd->hrs", queries, keys, preferred_element_type=jnp.float32) * scale
        visible = q_pos[:, None] >= k_pos[None, :]
        prob = jnp.where(visible[None], jnp.exp(score - stats[:, :, None]), 0.0)
        d_value = jnp.einsum(
            "hrs,rhd->sd", prob.astype(jnp.bfloat16), grad_out, preferred_element_type=jnp.float32
        )
        d_prob = jnp.einsum("rhd,sd->hrs", grad_out, values, preferred_element_type=jnp.float32)
        d_score = (prob * (d_prob - delta[:, :, None])).astype(jnp.bfloat16)
        d_query = (
            jnp.einsum("hrs,sd->rhd", d_score, keys, preferred_element_type=jnp.float32) * scale
        )
        d_key = (
            jnp.einsum("hrs,rhd->sd", d_score, queries, preferred_element_type=jnp.float32) * scale
        )
        return (d_query, jnp.stack([d_key, d_value]))

    pair = jnp.stack([key_rows[0], value_rows[0]])
    query_zero = jnp.zeros((rows, heads, head_dim), jnp.float32)

    def pass_grads(sums):
        return passed_along(sums, "ctx", 1)

    def cycle_step(step, carry):
        pair_now, sums, query_sum = carry
        owner = (mine - step) % width
        d_query, d_kv = tile(pair_now, slot_positions(block_order, owner, half))
        sums = pass_grads(sums + d_kv)
        pair_now = passed_along(pair_now, "ctx", 1)
        return (pair_now, sums, query_sum + d_query)

    start = (pair, jnp.zeros((2, rows, head_dim), jnp.float32), query_zero)
    pair_last, sums, query_sum = lax.fori_loop(0, width - 1, cycle_step, start)
    d_query, d_kv = tile(pair_last, slot_positions(block_order, (mine + 1) % width, half))
    kv_sums = pass_grads(sums + d_kv)
    query_sum = query_sum + d_query
    d_query_out = query_sum.reshape(1, rows, heads * head_dim).astype(jnp.bfloat16)
    grads_bf = jnp.concatenate([kv_sums[0], kv_sums[1]], axis=1).astype(jnp.bfloat16)
    inputs = layer_input[0]
    d_weight = lax.psum_scatter(
        lax.dot_general(
            inputs, grads_bf, (((0,), (0,)), ((), ())), preferred_element_type=jnp.float32
        ),
        ("dp", "ctx"),
        scatter_dimension=0,
        tiled=True,
    )
    return (d_query_out, d_weight)


def dot(left, right, contract=((1,), (0,))):
    return lax.dot_general(left, right, (contract, ((), ())), preferred_element_type=F32)


def fused_kernel(
    x_ref, q_hbm, k_hbm, v_hbm, o_hbm, do_hbm, lse_hbm, order_ref,
    dq_hbm, dw_ref,
    dq_ref, q_ref, o_ref, do_ref, lse_ref, xbuf, kv, lse2, delta, dq_acc, own, acc, g_send, g_recv, g_mine, g_other,
    a_keep, b_keep, a1_send, a1_recv, b1_send, b1_recv,
    a2_send, a2_recv, b2_send, b2_recv, last_keep, last_send, last_recv,
    x_local, x_send, x_recv, kv_ssem, kv_rsem, g_ssem, g_rsem,
    a1_ssem, a1_rsem, b1_ssem, b1_rsem, a2_ssem, a2_rsem, b2_ssem, b2_rsem,
    last_ssem, last_rsem, in_sem, dq_sem,
):
    rows, dh = k_hbm.shape[1], k_hbm.shape[2]
    heads = q_ref.shape[2] // dh
    half = rows // 2
    scale = dh ** (-0.5)
    dp, ctx = lax.axis_index("dp"), lax.axis_index("ctx")
    z, y = dp // 2, dp % 2
    x, c = ctx // 2, ctx % 2
    mate = (dp, 2 * x + 1 - c)
    side = (dp, 2 * (1 - x) + c)
    cross = (dp, 2 * (1 - x) + 1 - c)
    over = (2 * z + 1 - y, ctx)
    along = [(2 * ((z + k) % 4) + y, ctx) for k in (1, 2, 3)]

    loads = [
        pltpu.make_async_copy(source, target, in_sem.at[i])
        for i, (source, target) in enumerate(
            (
                (k_hbm.at[0], kv.at[0, :, pl.ds(0, dh)]),
                (v_hbm.at[0], kv.at[0, :, pl.ds(dh, dh)]),
                (do_hbm, do_ref),
                (o_hbm, o_ref),
                (q_hbm, q_ref),
                (lse_hbm, lse_ref),
            )
        )
    ]
    for copy in loads:
        copy.start()

    barrier = pltpu.get_barrier_semaphore()
    everyone = [mate, side, cross, over] + along
    for peer in everyone:
        pl.semaphore_signal(barrier, inc=1, device_id=peer, device_id_type=MESH)
    pl.semaphore_wait(barrier, len(everyone))
    loads[0].wait()
    loads[1].wait()

    started = []

    def send(source, target, ssem, rsem, peer):
        copy = pltpu.make_async_remote_copy(
            src_ref=source, dst_ref=target, send_sem=ssem, recv_sem=rsem,
            device_id=peer, device_id_type=MESH,
        )
        copy.start()
        started.append(copy)
        return copy

    kv_side = send(kv.at[0], kv.at[1], kv_ssem.at[0], kv_rsem.at[0], side)
    kv_mate = send(kv.at[0], kv.at[3], kv_ssem.at[2], kv_rsem.at[2], mate)

    def x_copies(m):
        mine = pl.ds(pl.multiple_of((2 * m + c) * rows, rows), rows)
        theirs = pl.ds(pl.multiple_of((2 * m + 1 - c) * rows, rows), rows)
        here = pltpu.make_async_copy(
            x_ref.at[0, :, mine], xbuf.at[m, pl.ds(0, rows), :], x_local.at[m]
        )
        there = pltpu.make_async_remote_copy(
            src_ref=x_ref.at[0, :, theirs], dst_ref=xbuf.at[m, pl.ds(rows, rows), :],
            send_sem=x_send.at[m], recv_sem=x_recv.at[m], device_id=mate, device_id_type=MESH,
        )
        return here, there

    @pl.loop(0, 16)
    def _(m):
        here, there = x_copies(m)
        there.start()
        here.start()

    for copy in loads[2:]:
        copy.wait()
    lse2[...] = lse_ref[0] * LOG2E

    @pl.loop(0, heads)
    def _(h):
        cols = pl.ds(pl.multiple_of(h * dh, dh), dh)
        product = do_ref[0, :, cols].astype(F32) * o_ref[0, :, cols].astype(F32)
        delta[pl.ds(h, 1), :] = jnp.sum(product.T, axis=0, keepdims=True)

    ahead = lax.broadcasted_iota(jnp.int32, (half, half), 1) - lax.broadcasted_iota(
        jnp.int32, (half, half), 0
    )

    def chunk(slot, owner, total, first):
        keys = kv[slot, :, 0:dh]
        values = kv[slot, :, dh : 2 * dh]
        keys_t = keys.astype(F32).T.astype(BF16)
        total[...] = jnp.zeros_like(total)

        def visible():
            return jnp.concatenate(
                [
                    jnp.concatenate(
                        [
                            ahead >= (order_ref[2 * owner + a] - order_ref[2 * ctx + b]) * half
                            for b in range(2)
                        ],
                        axis=1,
                    )
                    for a in range(2)
                ],
                axis=0,
            )

        def one(h):
            cols = pl.ds(h * dh, dh)
            query = q_ref[0, :, cols]
            grad = do_ref[0, :, cols]
            score = dot(keys, query, ((1,), (1,)))
            d_prob = dot(values, grad, ((1,), (1,)))
            prob = jnp.where(
                visible(), jnp.exp2(score * (scale * LOG2E) - lse2[pl.ds(h, 1), :]), 0.0
            )
            prob_b = prob.astype(BF16)
            d_score = (prob * (d_prob - delta[pl.ds(h, 1), :])).astype(BF16)
            d_value = dot(prob_b, grad)
            d_key = dot(d_score, query)
            d_query = dot(keys_t, d_score)
            if first:
                dq_acc[h] = d_query
            else:
                dq_acc[h] += d_query
            return d_key, d_value

        for h in range(heads):
            d_key, d_value = one(h)
            total[:, 0:dh] += d_key
            total[:, dh : 2 * dh] += d_value

    def give(slot, peer):
        g_send[slot - 1, :, 0:dh] = (acc[:, 0:dh] * scale).astype(BF16)
        g_send[slot - 1, :, dh : 2 * dh] = acc[:, dh : 2 * dh].astype(BF16)
        return send(
            g_send.at[slot - 1], g_recv.at[slot - 1], g_ssem.at[slot - 1], g_rsem.at[slot - 1], peer
        )

    chunk(0, ctx, own, True)
    kv_side.wait_recv()
    kv_cross = send(kv.at[1], kv.at[2], kv_ssem.at[1], kv_rsem.at[1], mate)
    chunk(1, side[1], acc, False)
    given = [give(1, side)]
    kv_cross.wait_recv()
    chunk(2, cross[1], acc, False)
    given.append(give(2, cross))
    kv_mate.wait_recv()
    chunk(3, mate[1], acc, False)
    given.append(give(3, mate))

    @pl.loop(0, heads)
    def _(h):
        cols = pl.ds(pl.multiple_of(h * dh, dh), dh)
        dq_ref[0, :, cols] = dq_acc[h].T

    dq_copy = pltpu.make_async_copy(dq_ref, dq_hbm, dq_sem.at[0])
    dq_copy.start()

    for copy in given:
        copy.wait_recv()
    d_key = own[:, 0:dh] * scale
    d_value = own[:, dh : 2 * dh]
    for slot in range(3):
        d_key = d_key + g_recv[slot, :, 0:dh].astype(F32)
        d_value = d_value + g_recv[slot, :, dh : 2 * dh].astype(F32)
    g_mine[0:dh, :] = d_key.T.astype(BF16)
    g_mine[dh : 2 * dh, :] = d_value.T.astype(BF16)
    g_copy = send(g_mine, g_other, g_ssem.at[3], g_rsem.at[3], mate)

    @pl.loop(0, 16)
    def _(m):
        here, there = x_copies(m)
        here.wait()
        there.wait()

    g_copy.wait_recv()

    first_a, first_b, second_a, second_b, final = {}, {}, {}, {}, {}

    def stage_one(k):
        strip = (z + k) % 4
        for yr in range(2):
            for xr in range(2):
                m = strip * 4 + (y + yr) % 2 * 2 + (x + xr) % 2
                part = dot(g_mine[...], xbuf[m, 0:rows, :]) + dot(
                    g_other[...], xbuf[m, rows : 2 * rows, :]
                )
                if xr:
                    a1_send[k, yr] = part[0:dh].astype(BF16)
                else:
                    a_keep[k, yr] = part[0:dh]
                if yr:
                    b1_send[k, xr] = part[dh : 2 * dh].astype(BF16)
                else:
                    b_keep[k, xr] = part[dh : 2 * dh]
        first_a[k] = send(a1_send.at[k], a1_recv.at[k], a1_ssem.at[k], a1_rsem.at[k], side)
        first_b[k] = send(b1_send.at[k], b1_recv.at[k], b1_ssem.at[k], b1_rsem.at[k], over)

    def stage_two(k):
        first_a[k].wait_recv()
        a2_send[k] = (a_keep[k, 1] + a1_recv[k, 1].astype(F32)).astype(BF16)
        second_a[k] = send(a2_send.at[k], a2_recv.at[k], a2_ssem.at[k], a2_rsem.at[k], over)
        first_b[k].wait_recv()
        b2_send[k] = (b_keep[k, 1] + b1_recv[k, 1].astype(F32)).astype(BF16)
        second_b[k] = send(b2_send.at[k], b2_recv.at[k], b2_ssem.at[k], b2_rsem.at[k], side)

    def stage_three(k):
        second_a[k].wait_recv()
        second_b[k].wait_recv()
        sum_a = a_keep[k, 0] + a1_recv[k, 0].astype(F32) + a2_recv[k].astype(F32)
        sum_b = b_keep[k, 0] + b1_recv[k, 0].astype(F32) + b2_recv[k].astype(F32)
        if k:
            last_send[k - 1, 0:dh, :] = sum_a.astype(BF16)
            last_send[k - 1, dh : 2 * dh, :] = sum_b.astype(BF16)
            final[k] = send(
                last_send.at[k - 1], last_recv.at[k - 1],
                last_ssem.at[k - 1], last_rsem.at[k - 1], along[k - 1],
            )
        else:
            last_keep[0:dh, :] = sum_a
            last_keep[dh : 2 * dh, :] = sum_b

    s = STRIPS
    stage_one(s[0])
    stage_one(s[1])
    stage_two(s[0])
    stage_one(s[2])
    stage_two(s[1])
    stage_three(s[0])
    stage_one(s[3])
    stage_two(s[2])
    stage_three(s[1])
    stage_two(s[3])
    stage_three(s[2])
    stage_three(s[3])
    for k in (1, 2, 3):
        final[k].wait_recv()
    result = last_keep[...]
    for k in range(3):
        result = result + last_recv[k].astype(F32)
    dw_ref[...] = result.T
    dq_copy.wait()
    for copy in started:
        copy.wait_send()


def fused_body(layer_input, query_rows, key_rows, value_rows, attn_out, d_attn, log_sum_exp, block_order):
    rows, dh = key_rows.shape[1], key_rows.shape[2]
    heads = query_rows.shape[2] // dh
    wide = 2 * dh
    vmem = pl.BlockSpec(memory_space=pltpu.VMEM)
    dma = pltpu.SemaphoreType.DMA
    d_query, d_weight = pl.pallas_call(
        fused_kernel,
        out_shape=(
            jax.ShapeDtypeStruct(query_rows.shape, F32),
            jax.ShapeDtypeStruct((rows, wide), F32),
        ),
        in_specs=[pl.BlockSpec(memory_space=pltpu.HBM)] * 7 + [pl.BlockSpec(memory_space=pltpu.SMEM)],
        out_specs=(pl.BlockSpec(memory_space=pltpu.HBM), vmem),
        scratch_shapes=[
            pltpu.VMEM(query_rows.shape, F32),
            pltpu.VMEM(query_rows.shape, BF16),
            pltpu.VMEM(query_rows.shape, BF16),
            pltpu.VMEM(query_rows.shape, BF16),
            pltpu.VMEM(log_sum_exp.shape, F32),
            pltpu.VMEM((16, 2 * rows, rows), BF16),
            pltpu.VMEM((4, rows, wide), BF16),
            pltpu.VMEM((heads, rows), F32),
            pltpu.VMEM((heads, rows), F32),
            pltpu.VMEM((heads, dh, rows), F32),
            pltpu.VMEM((rows, wide), F32),
            pltpu.VMEM((rows, wide), F32),
            pltpu.VMEM((3, rows, wide), BF16),
            pltpu.VMEM((3, rows, wide), BF16),
            pltpu.VMEM((wide, rows), BF16),
            pltpu.VMEM((wide, rows), BF16),
            pltpu.VMEM((4, 2, dh, rows), F32),
            pltpu.VMEM((4, 2, dh, rows), F32),
            pltpu.VMEM((4, 2, dh, rows), BF16),
            pltpu.VMEM((4, 2, dh, rows), BF16),
            pltpu.VMEM((4, 2, dh, rows), BF16),
            pltpu.VMEM((4, 2, dh, rows), BF16),
            pltpu.VMEM((4, dh, rows), BF16),
            pltpu.VMEM((4, dh, rows), BF16),
            pltpu.VMEM((4, dh, rows), BF16),
            pltpu.VMEM((4, dh, rows), BF16),
            pltpu.VMEM((wide, rows), F32),
            pltpu.VMEM((3, wide, rows), BF16),
            pltpu.VMEM((3, wide, rows), BF16),
            dma((16,)), dma((16,)), dma((16,)),
            dma((3,)), dma((3,)), dma((4,)), dma((4,)),
            dma((4,)), dma((4,)), dma((4,)), dma((4,)),
            dma((4,)), dma((4,)), dma((4,)), dma((4,)),
            dma((3,)), dma((3,)), dma((6,)), dma((1,)),
        ],
        compiler_params=pltpu.CompilerParams(
            collective_id=0, has_side_effects=True, vmem_limit_bytes=64 * 1024 * 1024
        ),
        cost_estimate=pl.CostEstimate(
            flops=4 * 10 * heads * rows * rows * dh + 4 * rows * rows * wide * 16,
            bytes_accessed=8 * 1024 * 1024,
            transcendentals=4 * heads * rows * rows,
        ),
    )(layer_input, query_rows, key_rows, value_rows, attn_out, d_attn, log_sum_exp, block_order)
    return (d_query * dh ** (-0.5)).astype(BF16), d_weight


def fits(mesh):
    return dict(mesh.shape) == {"dp": 8, "ctx": 4}


def solution(mesh):
    return jax.shard_map(
        fused_body if fits(mesh) else body,
        mesh=mesh,
        in_specs=(
            P("dp", "ctx", None),
            P("dp", "ctx", None),
            P("dp", "ctx", None),
            P("dp", "ctx", None),
            P("dp", "ctx", None),
            P("dp", "ctx", None),
            P("dp", None, "ctx"),
            P(),
        ),
        out_specs=(P("dp", "ctx", None), P(("dp", "ctx"), None)),
        check_vma=False,
    )
```

```python
import jax
import jax.numpy as jnp
from jax import lax
from jax.experimental import pallas as pl
from jax.experimental.pallas import tpu as pltpu
from jax.sharding import PartitionSpec as P

MESH = pl.DeviceIdType.MESH
F32 = jnp.float32
BF16 = jnp.bfloat16
LOG2E = 1.4426950408889634
STRIPS = (2, 1, 3, 0)


def passed_along(value, axis, steps):
    count = lax.axis_size(axis)
    pairs = [(source, (source + steps) % count) for source in range(count)]
    return lax.ppermute(value, axis, pairs)


def slot_positions(block_order, owner, half):
    firsts = lax.dynamic_slice_in_dim(block_order, 2 * owner, 2)
    offsets = jnp.arange(half, dtype=jnp.int32)
    return (firsts[:, None] * half + offsets[None, :]).reshape(2 * half)


def body(layer_input, query_rows, key_rows, value_rows, attn_out, d_attn, log_sum_exp, block_order):
    rows = query_rows.shape[1]
    head_dim = key_rows.shape[2]
    heads = query_rows.shape[2] // head_dim
    half = rows // 2
    scale = head_dim ** (-0.5)
    width = lax.axis_size("ctx")
    mine = lax.axis_index("ctx")
    q_pos = slot_positions(block_order, mine, half)
    queries = query_rows[0].reshape(rows, heads, head_dim)
    grad_out = d_attn[0].reshape(rows, heads, head_dim)
    saved = attn_out[0].reshape(rows, heads, head_dim)
    delta = jnp.sum(grad_out.astype(jnp.float32) * saved.astype(jnp.float32), axis=2).T
    stats = log_sum_exp[0]

    def tile(pair, k_pos):
        keys = pair[0]
        values = pair[1]
        score = jnp.einsum("rhd,sd->hrs", queries, keys, preferred_element_type=jnp.float32) * scale
        visible = q_pos[:, None] >= k_pos[None, :]
        prob = jnp.where(visible[None], jnp.exp(score - stats[:, :, None]), 0.0)
        d_value = jnp.einsum(
            "hrs,rhd->sd", prob.astype(jnp.bfloat16), grad_out, preferred_element_type=jnp.float32
        )
        d_prob = jnp.einsum("rhd,sd->hrs", grad_out, values, preferred_element_type=jnp.float32)
        d_score = (prob * (d_prob - delta[:, :, None])).astype(jnp.bfloat16)
        d_query = (
            jnp.einsum("hrs,sd->rhd", d_score, keys, preferred_element_type=jnp.float32) * scale
        )
        d_key = (
            jnp.einsum("hrs,rhd->sd", d_score, queries, preferred_element_type=jnp.float32) * scale
        )
        return (d_query, jnp.stack([d_key, d_value]))

    pair = jnp.stack([key_rows[0], value_rows[0]])
    query_zero = jnp.zeros((rows, heads, head_dim), jnp.float32)

    def pass_grads(sums):
        return passed_along(sums, "ctx", 1)

    def cycle_step(step, carry):
        pair_now, sums, query_sum = carry
        owner = (mine - step) % width
        d_query, d_kv = tile(pair_now, slot_positions(block_order, owner, half))
        sums = pass_grads(sums + d_kv)
        pair_now = passed_along(pair_now, "ctx", 1)
        return (pair_now, sums, query_sum + d_query)

    start = (pair, jnp.zeros((2, rows, head_dim), jnp.float32), query_zero)
    pair_last, sums, query_sum = lax.fori_loop(0, width - 1, cycle_step, start)
    d_query, d_kv = tile(pair_last, slot_positions(block_order, (mine + 1) % width, half))
    kv_sums = pass_grads(sums + d_kv)
    query_sum = query_sum + d_query
    d_query_out = query_sum.reshape(1, rows, heads * head_dim).astype(jnp.bfloat16)
    grads_bf = jnp.concatenate([kv_sums[0], kv_sums[1]], axis=1).astype(jnp.bfloat16)
    inputs = layer_input[0]
    d_weight = lax.psum_scatter(
        lax.dot_general(
            inputs, grads_bf, (((0,), (0,)), ((), ())), preferred_element_type=jnp.float32
        ),
        ("dp", "ctx"),
        scatter_dimension=0,
        tiled=True,
    )
    return (d_query_out, d_weight)


def dot(left, right, contract=((1,), (0,))):
    return lax.dot_general(left, right, (contract, ((), ())), preferred_element_type=F32)


def fused_kernel(
    x_ref, q_hbm, k_hbm, v_hbm, o_hbm, do_hbm, lse_hbm, order_ref,
    dq_hbm, dw_ref,
    dq_ref, q_ref, o_ref, do_ref, lse_ref, xbuf, kv, lse2, delta, dq_acc, own, acc, g_send, g_recv, g_mine, g_other,
    a_keep, b_keep, a1_send, a1_recv, b1_send, b1_recv,
    a2_send, a2_recv, b2_send, b2_recv, last_keep, last_send, last_recv,
    x_local, x_send, x_recv, kv_ssem, kv_rsem, g_ssem, g_rsem,
    a1_ssem, a1_rsem, b1_ssem, b1_rsem, a2_ssem, a2_rsem, b2_ssem, b2_rsem,
    last_ssem, last_rsem, in_sem, dq_sem,
):
    rows, dh = k_hbm.shape[1], k_hbm.shape[2]
    heads = q_ref.shape[2] // dh
    half = rows // 2
    scale = dh ** (-0.5)
    dp, ctx = lax.axis_index("dp"), lax.axis_index("ctx")
    z, y = dp // 2, dp % 2
    x, c = ctx // 2, ctx % 2
    mate = (dp, 2 * x + 1 - c)
    side = (dp, 2 * (1 - x) + c)
    cross = (dp, 2 * (1 - x) + 1 - c)
    over = (2 * z + 1 - y, ctx)
    along = [(2 * ((z + k) % 4) + y, ctx) for k in (1, 2, 3)]

    loads = [
        pltpu.make_async_copy(source, target, in_sem.at[i])
        for i, (source, target) in enumerate(
            (
                (k_hbm.at[0], kv.at[0, :, pl.ds(0, dh)]),
                (v_hbm.at[0], kv.at[0, :, pl.ds(dh, dh)]),
                (do_hbm, do_ref),
                (o_hbm, o_ref),
                (q_hbm, q_ref),
                (lse_hbm, lse_ref),
            )
        )
    ]
    for copy in loads:
        copy.start()

    barrier = pltpu.get_barrier_semaphore()
    everyone = [mate, side, cross, over] + along
    for peer in everyone:
        pl.semaphore_signal(barrier, inc=1, device_id=peer, device_id_type=MESH)
    pl.semaphore_wait(barrier, len(everyone))
    loads[0].wait()
    loads[1].wait()

    started = []

    def send(source, target, ssem, rsem, peer):
        copy = pltpu.make_async_remote_copy(
            src_ref=source, dst_ref=target, send_sem=ssem, recv_sem=rsem,
            device_id=peer, device_id_type=MESH,
        )
        copy.start()
        started.append(copy)
        return copy

    kv_side = send(kv.at[0], kv.at[1], kv_ssem.at[0], kv_rsem.at[0], side)
    kv_mate = send(kv.at[0], kv.at[3], kv_ssem.at[2], kv_rsem.at[2], mate)

    def x_copies(m):
        mine = pl.ds(pl.multiple_of((2 * m + c) * rows, rows), rows)
        theirs = pl.ds(pl.multiple_of((2 * m + 1 - c) * rows, rows), rows)
        here = pltpu.make_async_copy(
            x_ref.at[0, :, mine], xbuf.at[m, pl.ds(0, rows), :], x_local.at[m]
        )
        there = pltpu.make_async_remote_copy(
            src_ref=x_ref.at[0, :, theirs], dst_ref=xbuf.at[m, pl.ds(rows, rows), :],
            send_sem=x_send.at[m], recv_sem=x_recv.at[m], device_id=mate, device_id_type=MESH,
        )
        return here, there

    @pl.loop(0, 16)
    def _(m):
        here, there = x_copies(m)
        there.start()
        here.start()

    for copy in loads[2:]:
        copy.wait()
    lse2[...] = lse_ref[0] * LOG2E

    @pl.loop(0, heads)
    def _(h):
        cols = pl.ds(pl.multiple_of(h * dh, dh), dh)
        product = do_ref[0, :, cols].astype(F32) * o_ref[0, :, cols].astype(F32)
        delta[pl.ds(h, 1), :] = jnp.sum(product.T, axis=0, keepdims=True)

    ahead = lax.broadcasted_iota(jnp.int32, (half, half), 1) - lax.broadcasted_iota(
        jnp.int32, (half, half), 0
    )

    def chunk(slot, owner, total, first):
        keys = kv[slot, :, 0:dh]
        values = kv[slot, :, dh : 2 * dh]
        keys_t = keys.astype(F32).T.astype(BF16)
        total[...] = jnp.zeros_like(total)

        def visible():
            return jnp.concatenate(
                [
                    jnp.concatenate(
                        [
                            ahead >= (order_ref[2 * owner + a] - order_ref[2 * ctx + b]) * half
                            for b in range(2)
                        ],
                        axis=1,
                    )
                    for a in range(2)
                ],
                axis=0,
            )

        def one(h):
            cols = pl.ds(h * dh, dh)
            query = q_ref[0, :, cols]
            grad = do_ref[0, :, cols]
            score = dot(keys, query, ((1,), (1,)))
            d_prob = dot(values, grad, ((1,), (1,)))
            prob = jnp.where(
                visible(), jnp.exp2(score * (scale * LOG2E) - lse2[pl.ds(h, 1), :]), 0.0
            )
            prob_b = prob.astype(BF16)
            d_score = (prob * (d_prob - delta[pl.ds(h, 1), :])).astype(BF16)
            d_value = dot(prob_b, grad)
            d_key = dot(d_score, query)
            d_query = dot(keys_t, d_score)
            if first:
                dq_acc[h] = d_query
            else:
                dq_acc[h] += d_query
            return d_key, d_value

        for h in range(heads):
            d_key, d_value = one(h)
            total[:, 0:dh] += d_key
            total[:, dh : 2 * dh] += d_value

    def give(slot, peer):
        g_send[slot - 1, :, 0:dh] = (acc[:, 0:dh] * scale).astype(BF16)
        g_send[slot - 1, :, dh : 2 * dh] = acc[:, dh : 2 * dh].astype(BF16)
        return send(
            g_send.at[slot - 1], g_recv.at[slot - 1], g_ssem.at[slot - 1], g_rsem.at[slot - 1], peer
        )

    chunk(0, ctx, own, True)
    kv_side.wait_recv()
    kv_cross = send(kv.at[1], kv.at[2], kv_ssem.at[1], kv_rsem.at[1], mate)
    chunk(1, side[1], acc, False)
    given = [give(1, side)]
    kv_cross.wait_recv()
    chunk(2, cross[1], acc, False)
    given.append(give(2, cross))
    kv_mate.wait_recv()
    chunk(3, mate[1], acc, False)
    given.append(give(3, mate))

    @pl.loop(0, heads)
    def _(h):
        cols = pl.ds(pl.multiple_of(h * dh, dh), dh)
        dq_ref[0, :, cols] = (dq_acc[h] * scale).T.astype(BF16)

    dq_copy = pltpu.make_async_copy(dq_ref, dq_hbm, dq_sem.at[0])
    dq_copy.start()

    for copy in given:
        copy.wait_recv()
    d_key = own[:, 0:dh] * scale
    d_value = own[:, dh : 2 * dh]
    for slot in range(3):
        d_key = d_key + g_recv[slot, :, 0:dh].astype(F32)
        d_value = d_value + g_recv[slot, :, dh : 2 * dh].astype(F32)
    g_mine[0:dh, :] = d_key.T.astype(BF16)
    g_mine[dh : 2 * dh, :] = d_value.T.astype(BF16)
    g_copy = send(g_mine, g_other, g_ssem.at[3], g_rsem.at[3], mate)

    @pl.loop(0, 16)
    def _(m):
        here, there = x_copies(m)
        here.wait()
        there.wait()

    g_copy.wait_recv()

    first_a, first_b, second_a, second_b, final = {}, {}, {}, {}, {}

    def stage_one(k):
        strip = (z + k) % 4
        for yr in range(2):
            for xr in range(2):
                m = strip * 4 + (y + yr) % 2 * 2 + (x + xr) % 2
                part = dot(g_mine[...], xbuf[m, 0:rows, :]) + dot(
                    g_other[...], xbuf[m, rows : 2 * rows, :]
                )
                if xr:
                    a1_send[k, yr] = part[0:dh].astype(BF16)
                else:
                    a_keep[k, yr] = part[0:dh]
                if yr:
                    b1_send[k, xr] = part[dh : 2 * dh].astype(BF16)
                else:
                    b_keep[k, xr] = part[dh : 2 * dh]
        first_a[k] = send(a1_send.at[k], a1_recv.at[k], a1_ssem.at[k], a1_rsem.at[k], side)
        first_b[k] = send(b1_send.at[k], b1_recv.at[k], b1_ssem.at[k], b1_rsem.at[k], over)

    def stage_two(k):
        first_a[k].wait_recv()
        a2_send[k] = (a_keep[k, 1] + a1_recv[k, 1].astype(F32)).astype(BF16)
        second_a[k] = send(a2_send.at[k], a2_recv.at[k], a2_ssem.at[k], a2_rsem.at[k], over)
        first_b[k].wait_recv()
        b2_send[k] = (b_keep[k, 1] + b1_recv[k, 1].astype(F32)).astype(BF16)
        second_b[k] = send(b2_send.at[k], b2_recv.at[k], b2_ssem.at[k], b2_rsem.at[k], side)

    def stage_three(k):
        second_a[k].wait_recv()
        second_b[k].wait_recv()
        sum_a = a_keep[k, 0] + a1_recv[k, 0].astype(F32) + a2_recv[k].astype(F32)
        sum_b = b_keep[k, 0] + b1_recv[k, 0].astype(F32) + b2_recv[k].astype(F32)
        if k:
            last_send[k - 1, 0:dh, :] = sum_a.astype(BF16)
            last_send[k - 1, dh : 2 * dh, :] = sum_b.astype(BF16)
            final[k] = send(
                last_send.at[k - 1], last_recv.at[k - 1],
                last_ssem.at[k - 1], last_rsem.at[k - 1], along[k - 1],
            )
        else:
            last_keep[0:dh, :] = sum_a
            last_keep[dh : 2 * dh, :] = sum_b

    s = STRIPS
    stage_one(s[0])
    stage_one(s[1])
    stage_one(s[2])
    stage_two(s[0])
    stage_one(s[3])
    stage_two(s[1])
    stage_three(s[0])
    stage_two(s[2])
    stage_three(s[1])
    stage_two(s[3])
    stage_three(s[2])
    stage_three(s[3])
    for k in (1, 2, 3):
        final[k].wait_recv()
    result = last_keep[...]
    for k in range(3):
        result = result + last_recv[k].astype(F32)
    dw_ref[...] = result.T
    dq_copy.wait()
    for copy in started:
        copy.wait_send()


def fused_body(layer_input, query_rows, key_rows, value_rows, attn_out, d_attn, log_sum_exp, block_order):
    rows, dh = key_rows.shape[1], key_rows.shape[2]
    heads = query_rows.shape[2] // dh
    wide = 2 * dh
    vmem = pl.BlockSpec(memory_space=pltpu.VMEM)
    dma = pltpu.SemaphoreType.DMA
    return pl.pallas_call(
        fused_kernel,
        out_shape=(
            jax.ShapeDtypeStruct(query_rows.shape, BF16),
            jax.ShapeDtypeStruct((rows, wide), F32),
        ),
        in_specs=[pl.BlockSpec(memory_space=pltpu.HBM)] * 7 + [pl.BlockSpec(memory_space=pltpu.SMEM)],
        out_specs=(pl.BlockSpec(memory_space=pltpu.HBM), vmem),
        scratch_shapes=[
            pltpu.VMEM(query_rows.shape, BF16),
            pltpu.VMEM(query_rows.shape, BF16),
            pltpu.VMEM(query_rows.shape, BF16),
            pltpu.VMEM(query_rows.shape, BF16),
            pltpu.VMEM(log_sum_exp.shape, F32),
            pltpu.VMEM((16, 2 * rows, rows), BF16),
            pltpu.VMEM((4, rows, wide), BF16),
            pltpu.VMEM((heads, rows), F32),
            pltpu.VMEM((heads, rows), F32),
            pltpu.VMEM((heads, dh, rows), F32),
            pltpu.VMEM((rows, wide), F32),
            pltpu.VMEM((rows, wide), F32),
            pltpu.VMEM((3, rows, wide), BF16),
            pltpu.VMEM((3, rows, wide), BF16),
            pltpu.VMEM((wide, rows), BF16),
            pltpu.VMEM((wide, rows), BF16),
            pltpu.VMEM((4, 2, dh, rows), F32),
            pltpu.VMEM((4, 2, dh, rows), F32),
            pltpu.VMEM((4, 2, dh, rows), BF16),
            pltpu.VMEM((4, 2, dh, rows), BF16),
            pltpu.VMEM((4, 2, dh, rows), BF16),
            pltpu.VMEM((4, 2, dh, rows), BF16),
            pltpu.VMEM((4, dh, rows), BF16),
            pltpu.VMEM((4, dh, rows), BF16),
            pltpu.VMEM((4, dh, rows), BF16),
            pltpu.VMEM((4, dh, rows), BF16),
            pltpu.VMEM((wide, rows), F32),
            pltpu.VMEM((3, wide, rows), BF16),
            pltpu.VMEM((3, wide, rows), BF16),
            dma((16,)), dma((16,)), dma((16,)),
            dma((3,)), dma((3,)), dma((4,)), dma((4,)),
            dma((4,)), dma((4,)), dma((4,)), dma((4,)),
            dma((4,)), dma((4,)), dma((4,)), dma((4,)),
            dma((3,)), dma((3,)), dma((6,)), dma((1,)),
        ],
        compiler_params=pltpu.CompilerParams(
            collective_id=0, has_side_effects=True, vmem_limit_bytes=64 * 1024 * 1024
        ),
        cost_estimate=pl.CostEstimate(
            flops=4 * 10 * heads * rows * rows * dh + 4 * rows * rows * wide * 16,
            bytes_accessed=8 * 1024 * 1024,
            transcendentals=4 * heads * rows * rows,
        ),
    )(layer_input, query_rows, key_rows, value_rows, attn_out, d_attn, log_sum_exp, block_order)


def fits(mesh):
    return dict(mesh.shape) == {"dp": 8, "ctx": 4}


def solution(mesh):
    return jax.shard_map(
        fused_body if fits(mesh) else body,
        mesh=mesh,
        in_specs=(
            P("dp", "ctx", None),
            P("dp", "ctx", None),
            P("dp", "ctx", None),
            P("dp", "ctx", None),
            P("dp", "ctx", None),
            P("dp", "ctx", None),
            P("dp", None, "ctx"),
            P(),
        ),
        out_specs=(P("dp", "ctx", None), P(("dp", "ctx"), None)),
        check_vma=False,
    )
```
